32 devices in a mesh: rows: 32 (over z, y, x, core).
Axes of the slice: x: 2, y: 2, z: 4, core: 2. Of those that a mesh axis runs over, the one named last changes fastest.
Arguments:
- sketch: float32 [65536, 512], P('rows'), may hold values from -100 to 100
- panel: float32 [65536, 512], P('rows'), may hold values from -6 to 6
Outputs:
- basis: float32 [65536, 512], P('rows')
- projected: float32 [512, 512], P('rows')
The draws below stay inside these ranges and needn't reach their ends.
All inputs are finite; a program needn't handle non-finite values.
Results may differ from the reference program's by a relative error of at most 0.00029.
Values sent between devices are 32-bit elements; how exact they have to be, the bound alone decides.
A program may use at most 64 MiB of HBM per device.

```python
import jax
import jax.numpy as jnp
from jax import lax

K = 512
F = 512
ROWS = 65536


def draw_sketch(key, part):
    keys = jax.random.split(jax.random.fold_in(key, 7), 2)
    position = jnp.arange(ROWS, dtype=jnp.float32) / ROWS
    growth = jnp.exp(jnp.log(3.0) * position)[:, None]
    col_scale = jnp.exp(jax.random.uniform(keys[1], (1, K), jnp.float32, jnp.log(0.5), jnp.log(2.0)))
    base = jnp.clip(jax.random.normal(keys[0], (ROWS, K), jnp.float32), -6.0, 6.0)
    mixed = base + 0.6 * jnp.roll(base, 1, axis=1)
    values = mixed * col_scale * growth
    return jnp.clip(values, -100.0, 100.0).astype(jnp.float32)


def strengthened(result, own_key, source, target, blocks, factor):
    def block_of(dim):
        return (jnp.arange(result.shape[dim]) // (result.shape[dim] // blocks)).reshape((-1,) + (1,) * (result.ndim - 1 - dim))

    first = jax.random.permutation(own_key, blocks)[block_of(target)]
    other_side = (block_of(target) + blocks // 2) % blocks
    return jnp.where((block_of(source) == first) | (block_of(source) == other_side), factor * result, result)


def block_scale(stream_key, extent, cuts, low, largest):
    level = 1.0
    for axis_at, parts in cuts:
        heights = jax.random.uniform(jax.random.fold_in(jax.random.fold_in(stream_key, 6), axis_at), (parts,), jnp.float32, low / len(cuts), largest / len(cuts))
        level = level * jnp.repeat(jnp.exp(heights), extent[axis_at] // parts).reshape((-1,) + (1,) * (len(extent) - 1 - axis_at))
    return level


def bell_draw_with(stream_key, dims, spread, reach, pieces, heavy, kind=jnp.bfloat16):
    entries = spread * jax.random.normal(stream_key, dims, jnp.float32)
    if pieces:
        entries = entries * block_scale(stream_key, dims, pieces, -0.22, 0.18)
    return jnp.clip(strengthened(entries, jax.random.fold_in(stream_key, 3), *heavy), -reach, reach).astype(kind)


def setup_inputs(seed: int = 0) -> dict:
    arg_keys = jax.random.split(jax.random.key(seed), 3)
    sketch = draw_sketch(jax.random.fold_in(arg_keys[2], 71), 0)
    panel = bell_draw_with(arg_keys[1], (ROWS, F), 1.0, 6.0, ((0, 32),), (0, 1, 32, 2.75), jnp.float32)
    return {"sketch": sketch, "panel": panel}


def reference(sketch, panel):
    highest = lax.Precision.HIGHEST
    gram = lax.dot_general(sketch.astype(jnp.float32), sketch.astype(jnp.float32), (((0,), (0,)), ((), ())), precision=highest, preferred_element_type=jnp.float32) / ROWS
    lower = jnp.linalg.cholesky(gram)
    basis = jax.scipy.linalg.solve_triangular(lower, sketch.T, lower=True).T
    projected = lax.dot_general(panel.astype(jnp.float32), basis.astype(jnp.float32), (((0,), (0,)), ((), ())), precision=highest, preferred_element_type=jnp.float32)
    projected = projected / jnp.sqrt(jnp.float32(ROWS))
    return (basis, projected)
```

```python
import functools
import jax
import jax.numpy as jnp
from jax import lax
from jax.experimental import pallas as pl
from jax.experimental.pallas import tpu as pltpu
from jax.sharding import PartitionSpec as P

HI = lax.Precision.HIGHEST
BLK = 128
SUB = 8


def splat(x, i, j):
    return jnp.broadcast_to(x[i : i + 1, j : j + 1], (SUB, BLK))


def row(x, i):
    return jnp.broadcast_to(x[i : i + 1, :], (SUB, BLK))


def lane(x, j):
    return jnp.broadcast_to(x[:, j : j + 1], (SUB, BLK))


def small_inverse(a):
    n = SUB
    a = [list(r) for r in a]
    t = [[None] * n for _ in range(n)]
    for k in range(n):
        r = lax.rsqrt(a[k][k])
        l = {i: a[i][k] * r for i in range(k + 1, n)}
        for j in range(k + 1, n):
            for i in range(j, n):
                a[i][j] = a[i][j] - l[i] * l[j]
        t[k][k] = r
        for m in range(k):
            t[k][m] = t[k][m] * r
        for i in range(k + 1, n):
            for m in range(k + 1):
                e = l[i] * t[k][m]
                t[i][m] = -e if t[i][m] is None else t[i][m] - e
    return t


def block_inverse(a_ref, out_ref, base):
    lanes = lax.broadcasted_iota(jnp.int32, (SUB, BLK), 1)
    subs = lax.broadcasted_iota(jnp.int32, (SUB, BLK), 0)
    steps = BLK // SUB
    strips = [a_ref[i * SUB : (i + 1) * SUB, :] for i in range(steps)]
    for j in range(steps):
        j0 = j * SUB
        cur = strips[j]
        cols = [lane(cur, j0 + m) for m in range(SUB)]
        a = [[row(cols[m], i) for m in range(i + 1)] for i in range(SUB)]
        t = small_inverse(a)
        here = (lanes >= j0) & (lanes < j0 + SUB)
        mixed = jnp.where(here, jnp.where(lanes - j0 == subs, 1.0, 0.0), cur)
        rows = [row(mixed, m) for m in range(SUB)]
        r = []
        for k in range(SUB):
            acc = t[k][0] * rows[0]
            for m in range(1, k + 1):
                acc = acc + t[k][m] * rows[m]
            r.append(acc)
        if j + 1 < steps:
            q = []
            for k in range(SUB):
                acc = t[k][k] * r[k]
                for m in range(k + 1, SUB):
                    acc = acc + t[m][k] * r[m]
                q.append(acc)
            for i in range(j + 1, steps):
                x = strips[i]
                new = jnp.where(here, 0.0, x)
                for m in range(SUB):
                    new = new - lane(x, j0 + m) * q[m]
                strips[i] = new
        res = r[0]
        for k in range(1, SUB):
            res = jnp.where(subs == k, r[k], res)
        out_ref[j0 : j0 + SUB, :] = jnp.where(lanes <= j0 + subs, res, 0.0)


def inverse_factor(work, diag, dinv):
    n = work.shape[0]
    blocks = n // BLK
    ids = lax.broadcasted_iota(jnp.int32, (BLK, n), 1)
    subs = lax.broadcasted_iota(jnp.int32, (BLK, n), 0)

    def outer(p, c):
        at = pl.multiple_of(p * BLK, BLK)
        diag[...] = work[pl.ds(at, BLK), pl.ds(at, BLK)]
        block_inverse(diag, dinv, 0)
        work[pl.ds(at, BLK), pl.ds(at, BLK)] = jnp.where(
            lax.broadcasted_iota(jnp.int32, (BLK, BLK), 0) == lax.broadcasted_iota(jnp.int32, (BLK, BLK), 1), 1.0, 0.0)
        r = jnp.dot(dinv[...], work[pl.ds(at, BLK), :], precision=HI, preferred_element_type=jnp.float32)
        work[pl.ds(at, BLK), :] = r

        def update(q, c):
            to = pl.multiple_of(q * BLK, BLK)
            u = work[pl.ds(at, BLK), pl.ds(to, BLK)]
            work[pl.ds(to, BLK), pl.ds(at, BLK)] = jnp.zeros((BLK, BLK), jnp.float32)
            work[pl.ds(to, BLK), :] -= lax.dot_general(u, work[pl.ds(at, BLK), :], (((0,), (0,)), ((), ())), precision=HI, preferred_element_type=jnp.float32)
            return c

        lax.fori_loop(p + 1, blocks, update, 0)
        return c

    lax.fori_loop(0, blocks, outer, 0)


def split(x):
    hi = x.astype(jnp.bfloat16)
    return hi, (x - hi.astype(jnp.float32)).astype(jnp.bfloat16)


def over_rows(a, b):
    return lax.dot_general(a, b, (((0,), (0,)), ((), ())), preferred_element_type=jnp.float32)


def pairs(n):
    blocks = n // BLK
    return [(p, q) for p in range(blocks) for q in range(p, blocks)]


def sums_kernel(
    radices, s_hbm, p_hbm, full, share,
    s_buf, p_buf, gacc, g, g1, g2, g3, r, r1, r2, r3, in_sem,
    send_g, recv_g, send_r, recv_r, send_a, recv_a,
):
    ra, rb, rc = radices
    count = ra * rb * rc
    me = lax.axis_index("rows")
    a, b, c = lax.rem(me, ra), lax.rem(me // ra, rb), me // (ra * rb)
    k = s_buf.shape[1]
    rows = s_buf.shape[0]
    parts = in_sem.shape[1]
    step = rows // parts

    def load(t, i):
        src, dst = ((s_hbm, s_buf), (p_hbm, p_buf))[t]
        at = pl.ds(i * step, step)
        return pltpu.make_async_copy(src.at[at], dst.at[at], in_sem.at[t, i])

    for t in range(2):
        for i in range(parts):
            load(t, i).start()

    def device(x, y, z):
        return (x + ra * (y + rb * z),)

    def partner(stage, o):
        if stage == 0:
            d = lax.rem(a + o, ra)
            return device(d, b, c), d
        if stage == 1:
            d = lax.rem(b + o, rb)
            return device(a, d, c), d
        d = lax.rem(c + o, rc)
        return device(a, b, d), d

    barrier = pltpu.get_barrier_semaphore()
    for stage in range(3):
        for o in range(1, radices[stage]):
            pl.semaphore_signal(barrier, inc=1, device_id=partner(stage, o)[0], device_id_type=pl.DeviceIdType.MESH)

    digits = (a, b, c)

    def base_of(unit, stage):
        if stage == 0:
            return 0
        if stage == 1:
            return a * (rb * rc * unit)
        if stage == 2:
            return a * (rb * rc * unit) + b * (rc * unit)
        return a * (rb * rc * unit) + b * (rc * unit) + c * unit

    def width(unit, stage):
        return unit * (rb * rc, rc, 1)[stage]

    def reduce_copy(buf, recv, ss, rs, unit, stage, o, incoming):
        dev, d = partner(stage, o)
        w = width(unit, stage)
        at = pl.multiple_of(base_of(unit, stage) + d * w, 8)
        slot = d if incoming else digits[stage]
        return pltpu.make_async_remote_copy(
            src_ref=buf.at[pl.ds(at, w)], dst_ref=recv[stage].at[slot],
            send_sem=ss.at[stage, o], recv_sem=rs.at[stage, slot],
            device_id=dev, device_id_type=pl.DeviceIdType.MESH)

    def reduce_start(buf, recv, ss, rs, unit, stage):
        for o in range(1, radices[stage]):
            reduce_copy(buf, recv, ss, rs, unit, stage, o, False).start()

    def reduce_end(buf, recv, ss, rs, unit, stage, out=None):
        w = width(unit, stage)
        at = pl.ds(pl.multiple_of(base_of(unit, stage + 1), 8), w)
        total = buf[at, :]
        for o in range(1, radices[stage]):
            reduce_copy(buf, recv, ss, rs, unit, stage, o, True).wait_recv()
            total = total + recv[stage][partner(stage, o)[1]]
        if out is None:
            buf[at, :] = total
        else:
            out(total)
        for o in range(1, radices[stage]):
            reduce_copy(buf, recv, ss, rs, unit, stage, o, False).wait_send()

    def gather_copy(buf, ss, rs, unit, stage, o, incoming):
        dev, d = partner(stage, o)
        w = width(unit, stage)
        digit = d if incoming else digits[stage]
        at = pl.multiple_of(base_of(unit, stage) + digit * w, 8)
        return pltpu.make_async_remote_copy(
            src_ref=buf.at[pl.ds(at, w)], dst_ref=buf.at[pl.ds(at, w)],
            send_sem=ss.at[stage, o], recv_sem=rs.at[stage, digit],
            device_id=dev, device_id_type=pl.DeviceIdType.MESH)

    for i in range(parts):
        load(0, i).wait()
        hi, lo = split(s_buf[i * step : (i + 1) * step, :])
        both = over_rows(hi, jnp.concatenate([hi, lo], axis=1))
        if i == 0:
            gacc[...] = both
        else:
            gacc[...] += both
    inv = 1.0 / (rows * count)
    for n, (p, q) in enumerate(pairs(k)):
        rp, rq = slice(p * BLK, (p + 1) * BLK), slice(q * BLK, (q + 1) * BLK)
        mid = gacc[rp, k + q * BLK : k + (q + 1) * BLK]
        mir = gacc[rq, k + p * BLK : k + (p + 1) * BLK]
        g[n * BLK : (n + 1) * BLK, :] = (gacc[rp, rq] + (mid + mir.T)) * inv
    ug = g.shape[0] // count
    gr = (g, (g1, g2, g3), send_g, recv_g, ug)
    pl.semaphore_wait(barrier, ra + rb + rc - 3)
    reduce_start(*gr, 0)

    fr = p_buf.shape[1] // count
    for i in range(parts):
        load(1, i).wait()

    def product(f0):
        acc = None
        for i in range(parts):
            at = slice(i * step, (i + 1) * step)
            hi, lo = split(s_buf[at, :])
            ph, plo = split(p_buf[at, f0 : f0 + BLK])
            both = over_rows(ph, jnp.concatenate([hi, lo], axis=1))
            t = both[:, :k] + (both[:, k:] + over_rows(plo, hi))
            acc = t if acc is None else acc + t
        for m in range(BLK // fr):
            d = f0 // fr + m
            pos = (d % ra) * (rb * rc) + ((d // ra) % rb) * rc + d // (ra * rb)
            r[pos * fr : (pos + 1) * fr, :] = acc[m * fr : (m + 1) * fr, :]

    todo = list(range(0, p_buf.shape[1], BLK))
    product(todo[0])
    reduce_end(*gr, 0)
    reduce_start(*gr, 1)
    for f0 in todo[1:]:
        product(f0)
    reduce_end(*gr, 1)
    reduce_start(*gr, 2)
    rr = (r, (r1, r2, r3), send_r, recv_r, fr)
    reduce_start(*rr, 0)

    def put(total):
        full[pl.ds(pl.multiple_of(base_of(ug, 3), 8), ug), :] = total

    reduce_end(*gr, 2, put)

    def gather(stage, now):
        for o in range(1, radices[stage]):
            cp = gather_copy(full, send_a, recv_a, ug, stage, o, not now)
            if now:
                cp.start()
            else:
                cp.wait_recv()

    gather(2, True)
    reduce_end(*rr, 0)
    gather(2, False)
    gather(1, True)
    reduce_start(*rr, 1)
    gather(1, False)
    gather(0, True)
    reduce_end(*rr, 1)
    reduce_start(*rr, 2)
    gather(0, False)

    def put_share(total):
        share[...] = total

    reduce_end(*rr, 2, put_share)
    for stage in range(3):
        for o in range(1, radices[stage]):
            gather_copy(full, send_a, recv_a, ug, stage, o, False).wait_send()


def sums(sketch, panel, radices):
    rows, k = sketch.shape
    frames = panel.shape[1]
    ra, rb, rc = radices
    count = ra * rb * rc
    packed = len(pairs(k)) * BLK
    ug, ur = packed // count, frames // count
    parts = 4
    f32 = jnp.float32

    def slots(unit, width):
        return [
            pltpu.VMEM((ra, unit * rb * rc, width), f32),
            pltpu.VMEM((rb, unit * rc, width), f32),
            pltpu.VMEM((rc, unit, width), f32),
        ]

    most = max(radices)
    dma = pltpu.SemaphoreType.DMA
    return pl.pallas_call(
        functools.partial(sums_kernel, radices),
        out_shape=(jax.ShapeDtypeStruct((packed, BLK), f32), jax.ShapeDtypeStruct((ur, k), f32)),
        in_specs=[pl.BlockSpec(memory_space=pl.ANY)] * 2,
        out_specs=(pl.BlockSpec(memory_space=pltpu.VMEM),) * 2,
        scratch_shapes=[
            pltpu.VMEM((rows, k), f32), pltpu.VMEM((rows, frames), f32), pltpu.VMEM((k, 2 * k), f32),
            pltpu.VMEM((packed, BLK), f32), *slots(ug, BLK),
            pltpu.VMEM((frames, k), f32), *slots(ur, k),
            dma((2, parts)),
            dma((3, most)), dma((3, most)), dma((3, most)), dma((3, most)), dma((3, most)), dma((3, most)),
        ],
        compiler_params=pltpu.CompilerParams(
            collective_id=0, has_side_effects=True, vmem_limit_bytes=48 * 1024 * 1024),
    )(sketch, panel)


def basis_kernel(scale, g_ref, share_ref, s_ref, basis_ref, proj_ref, work, diag, dinv, wh, wl):
    n = work.shape[0]

    @pl.when(pl.program_id(0) == 0)
    def _():
        work[...] = jnp.zeros((n, n), jnp.float32)
        for i, (p, q) in enumerate(pairs(n)):
            work[p * BLK : (p + 1) * BLK, q * BLK : (q + 1) * BLK] = g_ref[i * BLK : (i + 1) * BLK, :]
        inverse_factor(work, diag, dinv)
        keep = lax.broadcasted_iota(jnp.int32, (n, n), 1) <= lax.broadcasted_iota(jnp.int32, (n, n), 0)
        w = jnp.where(keep, work[...], 0.0)
        hi, lo = split(w)
        wh[...] = hi
        wl[...] = lo
        proj_ref[...] = scale * lax.dot_general(
            share_ref[...], w, (((1,), (1,)), ((), ())), precision=HI, preferred_element_type=jnp.float32)

    def times(x, lo, hi, depth):
        nt = (((1,), (1,)), ((), ()))
        return lax.dot_general(x[:, :depth], lo[hi, :depth], nt, preferred_element_type=jnp.float32)

    sh, sl = split(s_ref[...])
    half = n // 2
    for at, depth in ((slice(0, half), half), (slice(half, n), n)):
        small = times(sh, wl, at, depth) + times(sl, wh, at, depth)
        basis_ref[:, at] = times(sh, wh, at, depth) + small


def finish(g, share, sketch, count):
    rows, k = sketch.shape
    tile = 256
    scale = 1.0 / (rows * count) ** 0.5
    f32 = jnp.float32
    return pl.pallas_call(
        functools.partial(basis_kernel, scale),
        grid=(rows // tile,),
        out_shape=(jax.ShapeDtypeStruct((rows, k), f32), jax.ShapeDtypeStruct(share.shape, f32)),
        in_specs=[
            pl.BlockSpec(g.shape, lambda i: (0, 0)),
            pl.BlockSpec(share.shape, lambda i: (0, 0)),
            pl.BlockSpec((tile, k), lambda i: (i, 0)),
        ],
        out_specs=(pl.BlockSpec((tile, k), lambda i: (i, 0)), pl.BlockSpec(share.shape, lambda i: (0, 0))),
        scratch_shapes=[
            pltpu.VMEM((k, k), f32), pltpu.VMEM((BLK, BLK), f32), pltpu.VMEM((BLK, BLK), f32),
            pltpu.VMEM((k, k), jnp.bfloat16), pltpu.VMEM((k, k), jnp.bfloat16),
        ],
        compiler_params=pltpu.CompilerParams(vmem_limit_bytes=32 * 1024 * 1024),
    )(g, share, sketch)


def plain_sums(sketch, panel):
    k = sketch.shape[1]
    total = sketch.shape[0] * lax.axis_size("rows")
    high = dict(precision=HI, preferred_element_type=jnp.float32)
    over = (((0,), (0,)), ((), ()))
    gram = lax.psum(lax.dot_general(sketch, sketch, over, **high) / total, "rows")
    share = lax.psum_scatter(lax.dot_general(panel, sketch, over, **high), "rows", scatter_dimension=0, tiled=True)
    blocks = [gram[p * BLK : (p + 1) * BLK, q * BLK : (q + 1) * BLK] for p, q in pairs(k)]
    return jnp.concatenate(blocks, axis=0), share


def on_device(sketch, panel):
    count = lax.axis_size("rows")
    k, frames = sketch.shape[1], panel.shape[1]
    packed = len(pairs(k)) * BLK
    if count % 8 == 0 and packed % (8 * count) == 0 and frames % (8 * count) == 0:
        g, share = sums(sketch, panel, (2, 4, count // 8))
    else:
        g, share = plain_sums(sketch, panel)
    return finish(g, share, sketch, count)


def solution(mesh):
    return jax.shard_map(
        on_device,
        mesh=mesh,
        in_specs=(P("rows", None), P("rows", None)),
        out_specs=(P("rows", None), P("rows", None)),
        check_vma=False,
    )
```

```python
import functools
import jax
import jax.numpy as jnp
from jax import lax
from jax.experimental import pallas as pl
from jax.experimental.pallas import tpu as pltpu
from jax.sharding import PartitionSpec as P

HI = lax.Precision.HIGHEST
BLK = 128
SUB = 8
GROUP = 64


def row(x, i):
    return jnp.broadcast_to(x[i : i + 1, :], (SUB, BLK))


def lane(x, j):
    return jnp.broadcast_to(x[:, j : j + 1], (SUB, BLK))


def small_inverse(a):
    n = SUB
    a = [list(r) for r in a]
    t = [[None] * n for _ in range(n)]
    for k in range(n):
        r = lax.rsqrt(a[k][k])
        l = {i: a[i][k] * r for i in range(k + 1, n)}
        for j in range(k + 1, n):
            for i in range(j, n):
                a[i][j] = a[i][j] - l[i] * l[j]
        t[k][k] = r
        for m in range(k):
            t[k][m] = t[k][m] * r
        for i in range(k + 1, n):
            for m in range(k + 1):
                e = l[i] * t[k][m]
                t[i][m] = -e if t[i][m] is None else t[i][m] - e
    return t


def block_inverse(a_ref, out_ref):
    lanes = lax.broadcasted_iota(jnp.int32, (SUB, BLK), 1)
    subs = lax.broadcasted_iota(jnp.int32, (SUB, BLK), 0)
    per = GROUP // SUB
    rest = a_ref[...]
    for g0 in range(0, BLK, GROUP):
        strips = [rest[i * SUB : (i + 1) * SUB, :] for i in range(per)]
        later = rest[GROUP:, :]
        done = []
        x = [row(strips[0], i) for i in range(SUB)]
        for j in range(per):
            j0 = g0 + j * SUB
            t = small_inverse([[lane(x[i], j0 + m) for m in range(i + 1)] for i in range(SUB)])
            here = (lanes >= j0) & (lanes < j0 + SUB)
            rows = [jnp.where(here, jnp.where(lanes == j0 + m, 1.0, 0.0), x[m]) for m in range(SUB)]
            near = j + 1 < per
            if near:
                c = [[lane(x[k], j0 + SUB + i) for k in range(SUB)] for i in range(SUB)]
                ahead = [jnp.where(here, 0.0, row(strips[j + 1], i)) for i in range(SUB)]
            r = []
            for k in range(SUB):
                acc = t[k][0] * rows[0]
                for m in range(1, k + 1):
                    acc = acc + t[k][m] * rows[m]
                r.append(acc)
            if near:
                q = []
                for k in range(SUB):
                    acc = t[SUB - 1][k] * r[SUB - 1]
                    for m in range(SUB - 2, k - 1, -1):
                        acc = acc + t[m][k] * r[m]
                    q.append(acc)
                x = []
                for i in range(SUB):
                    s0 = c[i][0] * q[0]
                    s1 = c[i][1] * q[1]
                    for m in range(2, SUB, 2):
                        s0 = s0 + c[i][m] * q[m]
                        s1 = s1 + c[i][m + 1] * q[m + 1]
                    x.append(ahead[i] - (s0 + s1))
                for i in range(j + 2, per):
                    old = strips[i]
                    strip = jnp.where(here, 0.0, old)
                    for m in range(SUB):
                        strip = strip - lane(old, j0 + m) * q[m]
                    strips[i] = strip
            res = r[0]
            for k in range(1, SUB):
                res = jnp.where(subs == k, r[k], res)
            done.append(res)
            out_ref[j0 : j0 + SUB, :] = jnp.where(lanes <= j0 + subs, res, 0.0)
        if g0 + GROUP < BLK:
            u = jnp.concatenate(done, axis=0)
            wide = lax.broadcasted_iota(jnp.int32, later.shape, 1)
            kept = jnp.where((wide >= g0) & (wide < g0 + GROUP), 0.0, later)
            own = lax.broadcasted_iota(jnp.int32, u.shape, 1) - g0
            dead = (own < GROUP) & (own > lax.broadcasted_iota(jnp.int32, u.shape, 0))
            full = lax.dot_general(u, jnp.where(dead, 0.0, u), (((0,), (0,)), ((), ())), precision=HI, preferred_element_type=jnp.float32)
            rest = kept - full[g0 + GROUP :, :]


def inverse_factor(work, diag, dinv, between=lambda p: None):
    n = work.shape[0]
    blocks = n // BLK
    ids = lax.broadcasted_iota(jnp.int32, (BLK, n), 1)
    subs = lax.broadcasted_iota(jnp.int32, (BLK, n), 0)

    def outer(p, c):
        at = pl.multiple_of(p * BLK, BLK)
        diag[...] = work[pl.ds(at, BLK), pl.ds(at, BLK)]
        block_inverse(diag, dinv)
        work[pl.ds(at, BLK), pl.ds(at, BLK)] = jnp.where(
            lax.broadcasted_iota(jnp.int32, (BLK, BLK), 0) == lax.broadcasted_iota(jnp.int32, (BLK, BLK), 1), 1.0, 0.0)
        r = jnp.dot(dinv[...], work[pl.ds(at, BLK), :], precision=HI, preferred_element_type=jnp.float32)
        work[pl.ds(at, BLK), :] = r

        def update(q, c):
            to = pl.multiple_of(q * BLK, BLK)
            u = work[pl.ds(at, BLK), pl.ds(to, BLK)]
            work[pl.ds(to, BLK), pl.ds(at, BLK)] = jnp.zeros((BLK, BLK), jnp.float32)
            work[pl.ds(to, BLK), :] -= lax.dot_general(u, work[pl.ds(at, BLK), :], (((0,), (0,)), ((), ())), precision=HI, preferred_element_type=jnp.float32)
            return c

        lax.fori_loop(p + 1, blocks, update, 0)
        between(p)
        return c

    lax.fori_loop(0, blocks, outer, 0)


def split(x):
    hi = x.astype(jnp.bfloat16)
    return hi, (x - hi.astype(jnp.float32)).astype(jnp.bfloat16)


def over_rows(a, b):
    return lax.dot_general(a, b, (((0,), (0,)), ((), ())), preferred_element_type=jnp.float32)


def pairs(n):
    blocks = n // BLK
    return [(p, q) for p in range(blocks) for q in range(p, blocks)]


def sums_kernel(
    radices, s_hbm, p_hbm, inverse, share,
    work, diag, dinv, full, s_buf, p_buf, gacc, g, g1, g2, g3, r, r1, r2, r3, in_sem,
    send_g, recv_g, send_r, recv_r, send_a, recv_a,
):
    ra, rb, rc = radices
    count = ra * rb * rc
    me = lax.axis_index("rows")
    a, b, c = lax.rem(me, ra), lax.rem(me // ra, rb), me // (ra * rb)
    k = s_buf.shape[1]
    rows = s_buf.shape[0]
    parts = in_sem.shape[1]
    step = rows // parts

    def load(t, i):
        src, dst = ((s_hbm, s_buf), (p_hbm, p_buf))[t]
        at = pl.ds(i * step, step)
        return pltpu.make_async_copy(src.at[at], dst.at[at], in_sem.at[t, i])

    for t in range(2):
        for i in range(parts):
            load(t, i).start()

    def device(x, y, z):
        return (x + ra * (y + rb * z),)

    def partner(stage, o):
        if stage == 0:
            d = lax.rem(a + o, ra)
            return device(d, b, c), d
        if stage == 1:
            d = lax.rem(b + o, rb)
            return device(a, d, c), d
        d = lax.rem(c + o, rc)
        return device(a, b, d), d

    barrier = pltpu.get_barrier_semaphore()
    for stage in range(3):
        for o in range(1, radices[stage]):
            pl.semaphore_signal(barrier, inc=1, device_id=partner(stage, o)[0], device_id_type=pl.DeviceIdType.MESH)

    digits = (a, b, c)

    def base_of(unit, stage):
        if stage == 0:
            return 0
        if stage == 1:
            return a * (rb * rc * unit)
        if stage == 2:
            return a * (rb * rc * unit) + b * (rc * unit)
        return a * (rb * rc * unit) + b * (rc * unit) + c * unit

    def width(unit, stage):
        return unit * (rb * rc, rc, 1)[stage]

    def reduce_copy(buf, recv, ss, rs, unit, stage, o, incoming):
        dev, d = partner(stage, o)
        w = width(unit, stage)
        at = pl.multiple_of(base_of(unit, stage) + d * w, 8)
        slot = d if incoming else digits[stage]
        return pltpu.make_async_remote_copy(
            src_ref=buf.at[pl.ds(at, w)], dst_ref=recv[stage].at[slot],
            send_sem=ss.at[stage, o], recv_sem=rs.at[stage, slot],
            device_id=dev, device_id_type=pl.DeviceIdType.MESH)

    def reduce_start(buf, recv, ss, rs, unit, stage):
        for o in range(1, radices[stage]):
            reduce_copy(buf, recv, ss, rs, unit, stage, o, False).start()

    def reduce_end(buf, recv, ss, rs, unit, stage, out=None):
        w = width(unit, stage)
        at = pl.ds(pl.multiple_of(base_of(unit, stage + 1), 8), w)
        total = buf[at, :]
        for o in range(1, radices[stage]):
            reduce_copy(buf, recv, ss, rs, unit, stage, o, True).wait_recv()
            total = total + recv[stage][partner(stage, o)[1]]
        if out is None:
            buf[at, :] = total
        else:
            out(total)
        for o in range(1, radices[stage]):
            reduce_copy(buf, recv, ss, rs, unit, stage, o, False).wait_send()

    def gather_copy(buf, ss, rs, unit, stage, o, incoming):
        dev, d = partner(stage, o)
        w = width(unit, stage)
        digit = d if incoming else digits[stage]
        at = pl.multiple_of(base_of(unit, stage) + digit * w, 8)
        return pltpu.make_async_remote_copy(
            src_ref=buf.at[pl.ds(at, w)], dst_ref=buf.at[pl.ds(at, w)],
            send_sem=ss.at[stage, o], recv_sem=rs.at[stage, digit],
            device_id=dev, device_id_type=pl.DeviceIdType.MESH)

    for i in range(parts):
        load(0, i).wait()
        hi, lo = split(s_buf[i * step : (i + 1) * step, :])
        both = over_rows(hi, jnp.concatenate([hi, lo], axis=1))
        if i == 0:
            gacc[...] = both
        else:
            gacc[...] += both
    inv = 1.0 / (rows * count)
    for n, (p, q) in enumerate(pairs(k)):
        rp, rq = slice(p * BLK, (p + 1) * BLK), slice(q * BLK, (q + 1) * BLK)
        mid = gacc[rp, k + q * BLK : k + (q + 1) * BLK]
        mir = gacc[rq, k + p * BLK : k + (p + 1) * BLK]
        g[n * BLK : (n + 1) * BLK, :] = (gacc[rp, rq] + (mid + mir.T)) * inv
    ug = g.shape[0] // count
    gr = (g, (g1, g2, g3), send_g, recv_g, ug)
    pl.semaphore_wait(barrier, ra + rb + rc - 3)
    reduce_start(*gr, 0)

    fr = p_buf.shape[1] // count
    for i in range(parts):
        load(1, i).wait()

    def product(f0):
        acc = None
        for i in range(parts):
            at = slice(i * step, (i + 1) * step)
            hi, lo = split(s_buf[at, :])
            ph, plo = split(p_buf[at, f0 : f0 + BLK])
            both = over_rows(ph, jnp.concatenate([hi, lo], axis=1))
            t = both[:, :k] + (both[:, k:] + over_rows(plo, hi))
            acc = t if acc is None else acc + t
        for m in range(BLK // fr):
            d = f0 // fr + m
            pos = (d % ra) * (rb * rc) + ((d // ra) % rb) * rc + d // (ra * rb)
            r[pos * fr : (pos + 1) * fr, :] = acc[m * fr : (m + 1) * fr, :]

    todo = list(range(0, p_buf.shape[1], BLK))
    product(todo[0])
    reduce_end(*gr, 0)
    reduce_start(*gr, 1)
    for f0 in todo[1:]:
        product(f0)
    reduce_end(*gr, 1)
    reduce_start(*gr, 2)
    rr = (r, (r1, r2, r3), send_r, recv_r, fr)

    def put(total):
        full[pl.ds(pl.multiple_of(base_of(ug, 3), 8), ug), :] = total

    reduce_end(*gr, 2, put)

    def gather(stage, now):
        for o in range(1, radices[stage]):
            cp = gather_copy(full, send_a, recv_a, ug, stage, o, not now)
            if now:
                cp.start()
            else:
                cp.wait_recv()

    for stage in (2, 1, 0):
        gather(stage, True)
        gather(stage, False)

    reduce_start(*rr, 0)
    work[...] = jnp.zeros((k, k), jnp.float32)
    for i, (p, q) in enumerate(pairs(k)):
        work[p * BLK : (p + 1) * BLK, q * BLK : (q + 1) * BLK] = full[i * BLK : (i + 1) * BLK, :]

    def put_share(total):
        share[...] = total

    def between(p):
        @pl.when(p == 0)
        def _():
            reduce_end(*rr, 0)
            reduce_start(*rr, 1)

        @pl.when(p == 1)
        def _():
            reduce_end(*rr, 1)
            reduce_start(*rr, 2)

    inverse_factor(work, diag, dinv, between)
    reduce_end(*rr, 2, put_share)
    keep = lax.broadcasted_iota(jnp.int32, (k, k), 1) <= lax.broadcasted_iota(jnp.int32, (k, k), 0)
    inverse[...] = jnp.where(keep, work[...], 0.0)
    for stage in range(3):
        for o in range(1, radices[stage]):
            gather_copy(full, send_a, recv_a, ug, stage, o, False).wait_send()


def sums(sketch, panel, radices):
    rows, k = sketch.shape
    frames = panel.shape[1]
    ra, rb, rc = radices
    count = ra * rb * rc
    packed = len(pairs(k)) * BLK
    ug, ur = packed // count, frames // count
    parts = 4
    f32 = jnp.float32

    def slots(unit, width):
        return [
            pltpu.VMEM((ra, unit * rb * rc, width), f32),
            pltpu.VMEM((rb, unit * rc, width), f32),
            pltpu.VMEM((rc, unit, width), f32),
        ]

    most = max(radices)
    dma = pltpu.SemaphoreType.DMA
    return pl.pallas_call(
        functools.partial(sums_kernel, radices),
        out_shape=(jax.ShapeDtypeStruct((k, k), f32), jax.ShapeDtypeStruct((ur, k), f32)),
        in_specs=[pl.BlockSpec(memory_space=pl.ANY)] * 2,
        out_specs=(pl.BlockSpec(memory_space=pltpu.VMEM),) * 2,
        scratch_shapes=[
            pltpu.VMEM((k, k), f32), pltpu.VMEM((BLK, BLK), f32), pltpu.VMEM((BLK, BLK), f32),
            pltpu.VMEM((packed, BLK), f32),
            pltpu.VMEM((rows, k), f32), pltpu.VMEM((rows, frames), f32), pltpu.VMEM((k, 2 * k), f32),
            pltpu.VMEM((packed, BLK), f32), *slots(ug, BLK),
            pltpu.VMEM((frames, k), f32), *slots(ur, k),
            dma((2, parts)),
            dma((3, most)), dma((3, most)), dma((3, most)), dma((3, most)), dma((3, most)), dma((3, most)),
        ],
        compiler_params=pltpu.CompilerParams(
            collective_id=0, has_side_effects=True, vmem_limit_bytes=60 * 1024 * 1024),
    )(sketch, panel)


def factor_kernel(g_ref, inverse, work, diag, dinv):
    k = work.shape[0]
    work[...] = jnp.zeros((k, k), jnp.float32)
    for i, (p, q) in enumerate(pairs(k)):
        work[p * BLK : (p + 1) * BLK, q * BLK : (q + 1) * BLK] = g_ref[i * BLK : (i + 1) * BLK, :]
    inverse_factor(work, diag, dinv)
    keep = lax.broadcasted_iota(jnp.int32, (k, k), 1) <= lax.broadcasted_iota(jnp.int32, (k, k), 0)
    inverse[...] = jnp.where(keep, work[...], 0.0)


def factor(g, k):
    f32 = jnp.float32
    return pl.pallas_call(
        factor_kernel,
        out_shape=jax.ShapeDtypeStruct((k, k), f32),
        scratch_shapes=[pltpu.VMEM((k, k), f32), pltpu.VMEM((BLK, BLK), f32), pltpu.VMEM((BLK, BLK), f32)],
        compiler_params=pltpu.CompilerParams(vmem_limit_bytes=32 * 1024 * 1024),
    )(g)


def basis_kernel(scale, w_ref, share_ref, s_ref, basis_ref, proj_ref, wh, wl):
    n = w_ref.shape[0]

    @pl.when(pl.program_id(0) == 0)
    def _():
        w = w_ref[...]
        hi, lo = split(w)
        wh[...] = hi
        wl[...] = lo
        proj_ref[...] = scale * lax.dot_general(
            share_ref[...], w, (((1,), (1,)), ((), ())), precision=HI, preferred_element_type=jnp.float32)

    def times(x, lo, hi, depth):
        nt = (((1,), (1,)), ((), ()))
        return lax.dot_general(x[:, :depth], lo[hi, :depth], nt, preferred_element_type=jnp.float32)

    sh, sl = split(s_ref[...])
    half = n // 2
    for at, depth in ((slice(0, half), half), (slice(half, n), n)):
        small = times(sh, wl, at, depth) + times(sl, wh, at, depth)
        basis_ref[:, at] = times(sh, wh, at, depth) + small


def finish(w, share, sketch, count):
    rows, k = sketch.shape
    tile = 256
    scale = 1.0 / (rows * count) ** 0.5
    f32 = jnp.float32
    return pl.pallas_call(
        functools.partial(basis_kernel, scale),
        grid=(rows // tile,),
        out_shape=(jax.ShapeDtypeStruct((rows, k), f32), jax.ShapeDtypeStruct(share.shape, f32)),
        in_specs=[
            pl.BlockSpec(w.shape, lambda i: (0, 0)),
            pl.BlockSpec(share.shape, lambda i: (0, 0)),
            pl.BlockSpec((tile, k), lambda i: (i, 0)),
        ],
        out_specs=(pl.BlockSpec((tile, k), lambda i: (i, 0)), pl.BlockSpec(share.shape, lambda i: (0, 0))),
        scratch_shapes=[
            pltpu.VMEM((k, k), jnp.bfloat16), pltpu.VMEM((k, k), jnp.bfloat16),
        ],
        compiler_params=pltpu.CompilerParams(vmem_limit_bytes=60 * 1024 * 1024),
    )(w, share, sketch)


def plain_sums(sketch, panel):
    k = sketch.shape[1]
    total = sketch.shape[0] * lax.axis_size("rows")
    high = dict(precision=HI, preferred_element_type=jnp.float32)
    over = (((0,), (0,)), ((), ()))
    gram = lax.psum(lax.dot_general(sketch, sketch, over, **high) / total, "rows")
    share = lax.psum_scatter(lax.dot_general(panel, sketch, over, **high), "rows", scatter_dimension=0, tiled=True)
    blocks = [gram[p * BLK : (p + 1) * BLK, q * BLK : (q + 1) * BLK] for p, q in pairs(k)]
    return jnp.concatenate(blocks, axis=0), share


def on_device(sketch, panel):
    count = lax.axis_size("rows")
    k, frames = sketch.shape[1], panel.shape[1]
    packed = len(pairs(k)) * BLK
    if count % 8 == 0 and packed % (8 * count) == 0 and frames % (8 * count) == 0:
        w, share = sums(sketch, panel, (2, 4, count // 8))
    else:
        g, share = plain_sums(sketch, panel)
        w = factor(g, k)
    return finish(w, share, sketch, count)


def solution(mesh):
    return jax.shard_map(
        on_device,
        mesh=mesh,
        in_specs=(P("rows", None), P("rows", None)),
        out_specs=(P("rows", None), P("rows", None)),
        check_vma=False,
    )
```

```python
import functools
import jax
import jax.numpy as jnp
from jax import lax
from jax.experimental import pallas as pl
from jax.experimental.pallas import tpu as pltpu
from jax.sharding import PartitionSpec as P

HI = lax.Precision.HIGHEST
BLK = 128
SUB = 8
GROUP = 64


def row(x, i):
    return jnp.broadcast_to(x[i : i + 1, :], (SUB, BLK))


def lane(x, j):
    return jnp.broadcast_to(x[:, j : j + 1], (SUB, BLK))


def small_inverse(a):
    n = SUB
    a = [list(r) for r in a]
    t = [[None] * n for _ in range(n)]
    for k in range(n):
        r = lax.rsqrt(a[k][k])
        l = {i: a[i][k] * r for i in range(k + 1, n)}
        for j in range(k + 1, n):
            for i in range(j, n):
                a[i][j] = a[i][j] - l[i] * l[j]
        t[k][k] = r
        for m in range(k):
            t[k][m] = t[k][m] * r
        for i in range(k + 1, n):
            for m in range(k + 1):
                e = l[i] * t[k][m]
                t[i][m] = -e if t[i][m] is None else t[i][m] - e
    return t


def block_inverse(a_ref, out_ref):
    lanes = lax.broadcasted_iota(jnp.int32, (SUB, BLK), 1)
    subs = lax.broadcasted_iota(jnp.int32, (SUB, BLK), 0)
    per = GROUP // SUB
    rest = a_ref[...]
    for g0 in range(0, BLK, GROUP):
        strips = [rest[i * SUB : (i + 1) * SUB, :] for i in range(per)]
        later = rest[GROUP:, :]
        done = []
        x = [row(strips[0], i) for i in range(SUB)]
        for j in range(per):
            j0 = g0 + j * SUB
            t = small_inverse([[lane(x[i], j0 + m) for m in range(i + 1)] for i in range(SUB)])
            here = (lanes >= j0) & (lanes < j0 + SUB)
            rows = [jnp.where(here, jnp.where(lanes == j0 + m, 1.0, 0.0), x[m]) for m in range(SUB)]
            near = j + 1 < per
            if near:
                c = [[lane(x[k], j0 + SUB + i) for k in range(SUB)] for i in range(SUB)]
                ahead = [jnp.where(here, 0.0, row(strips[j + 1], i)) for i in range(SUB)]
            r = []
            for k in range(SUB):
                acc = t[k][0] * rows[0]
                for m in range(1, k + 1):
                    acc = acc + t[k][m] * rows[m]
                r.append(acc)
            if near:
                q = []
                for k in range(SUB):
                    acc = t[SUB - 1][k] * r[SUB - 1]
                    for m in range(SUB - 2, k - 1, -1):
                        acc = acc + t[m][k] * r[m]
                    q.append(acc)
                x = []
                for i in range(SUB):
                    s0 = c[i][0] * q[0]
                    s1 = c[i][1] * q[1]
                    for m in range(2, SUB, 2):
                        s0 = s0 + c[i][m] * q[m]
                        s1 = s1 + c[i][m + 1] * q[m + 1]
                    x.append(ahead[i] - (s0 + s1))
                for i in range(j + 2, per):
                    old = strips[i]
                    strip = jnp.where(here, 0.0, old)
                    for m in range(SUB):
                        strip = strip - lane(old, j0 + m) * q[m]
                    strips[i] = strip
            res = r[0]
            for k in range(1, SUB):
                res = jnp.where(subs == k, r[k], res)
            done.append(res)
            out_ref[j0 : j0 + SUB, :] = jnp.where(lanes <= j0 + subs, res, 0.0)
        if g0 + GROUP < BLK:
            u = jnp.concatenate(done, axis=0)
            wide = lax.broadcasted_iota(jnp.int32, later.shape, 1)
            kept = jnp.where((wide >= g0) & (wide < g0 + GROUP), 0.0, later)
            own = lax.broadcasted_iota(jnp.int32, u.shape, 1) - g0
            dead = (own < GROUP) & (own > lax.broadcasted_iota(jnp.int32, u.shape, 0))
            full = lax.dot_general(u, jnp.where(dead, 0.0, u), (((0,), (0,)), ((), ())), precision=HI, preferred_element_type=jnp.float32)
            rest = kept - full[g0 + GROUP :, :]


def inverse_factor(work, diag, dinv, between=lambda p: None):
    n = work.shape[0]
    blocks = n // BLK
    ids = lax.broadcasted_iota(jnp.int32, (BLK, n), 1)
    subs = lax.broadcasted_iota(jnp.int32, (BLK, n), 0)

    def outer(p, c):
        at = pl.multiple_of(p * BLK, BLK)
        diag[...] = work[pl.ds(at, BLK), pl.ds(at, BLK)]
        block_inverse(diag, dinv)
        work[pl.ds(at, BLK), pl.ds(at, BLK)] = jnp.where(
            lax.broadcasted_iota(jnp.int32, (BLK, BLK), 0) == lax.broadcasted_iota(jnp.int32, (BLK, BLK), 1), 1.0, 0.0)
        r = jnp.dot(dinv[...], work[pl.ds(at, BLK), :], precision=HI, preferred_element_type=jnp.float32)
        work[pl.ds(at, BLK), :] = r

        def update(q, c):
            to = pl.multiple_of(q * BLK, BLK)
            u = work[pl.ds(at, BLK), pl.ds(to, BLK)]
            work[pl.ds(to, BLK), pl.ds(at, BLK)] = jnp.zeros((BLK, BLK), jnp.float32)
            work[pl.ds(to, BLK), :] -= lax.dot_general(u, work[pl.ds(at, BLK), :], (((0,), (0,)), ((), ())), precision=HI, preferred_element_type=jnp.float32)
            return c

        lax.fori_loop(p + 1, blocks, update, 0)
        between(p)
        return c

    lax.fori_loop(0, blocks, outer, 0)


def split(x):
    hi = x.astype(jnp.bfloat16)
    return hi, (x - hi.astype(jnp.float32)).astype(jnp.bfloat16)


def over_rows(a, b):
    return lax.dot_general(a, b, (((0,), (0,)), ((), ())), preferred_element_type=jnp.float32)


def pairs(n):
    blocks = n // BLK
    return [(p, q) for p in range(blocks) for q in range(p, blocks)]


def sums_kernel(
    radices, s_hbm, p_hbm, inverse, share,
    work, diag, dinv, full, s_buf, p_buf, gacc, g, g1, g2, g3, r, r1, r2, r3, in_sem,
    send_g, recv_g, send_r, recv_r, send_a, recv_a,
):
    ra, rb, rc = radices
    count = ra * rb * rc
    me = lax.axis_index("rows")
    a, b, c = lax.rem(me, ra), lax.rem(me // ra, rb), me // (ra * rb)
    k = s_buf.shape[1]
    rows = s_buf.shape[0]
    parts = in_sem.shape[1]
    step = rows // parts

    def load(t, i):
        src, dst = ((s_hbm, s_buf), (p_hbm, p_buf))[t]
        at = pl.ds(i * step, step)
        return pltpu.make_async_copy(src.at[at], dst.at[at], in_sem.at[t, i])

    for t in range(2):
        for i in range(parts):
            load(t, i).start()

    def device(x, y, z):
        return (x + ra * (y + rb * z),)

    def partner(stage, o):
        if stage == 0:
            d = lax.rem(a + o, ra)
            return device(d, b, c), d
        if stage == 1:
            d = lax.rem(b + o, rb)
            return device(a, d, c), d
        d = lax.rem(c + o, rc)
        return device(a, b, d), d

    barrier = pltpu.get_barrier_semaphore()
    for stage in range(3):
        for o in range(1, radices[stage]):
            pl.semaphore_signal(barrier, inc=1, device_id=partner(stage, o)[0], device_id_type=pl.DeviceIdType.MESH)

    digits = (a, b, c)

    def base_of(unit, stage):
        if stage == 0:
            return 0
        if stage == 1:
            return a * (rb * rc * unit)
        if stage == 2:
            return a * (rb * rc * unit) + b * (rc * unit)
        return a * (rb * rc * unit) + b * (rc * unit) + c * unit

    def width(unit, stage):
        return unit * (rb * rc, rc, 1)[stage]

    def reduce_copy(buf, recv, ss, rs, unit, stage, o, incoming):
        dev, d = partner(stage, o)
        w = width(unit, stage)
        at = pl.multiple_of(base_of(unit, stage) + d * w, 8)
        slot = d if incoming else digits[stage]
        return pltpu.make_async_remote_copy(
            src_ref=buf.at[pl.ds(at, w)], dst_ref=recv[stage].at[slot],
            send_sem=ss.at[stage, o], recv_sem=rs.at[stage, slot],
            device_id=dev, device_id_type=pl.DeviceIdType.MESH)

    def reduce_start(buf, recv, ss, rs, unit, stage):
        for o in range(1, radices[stage]):
            reduce_copy(buf, recv, ss, rs, unit, stage, o, False).start()

    def reduce_end(buf, recv, ss, rs, unit, stage, out=None):
        w = width(unit, stage)
        at = pl.ds(pl.multiple_of(base_of(unit, stage + 1), 8), w)
        total = buf[at, :]
        for o in range(1, radices[stage]):
            reduce_copy(buf, recv, ss, rs, unit, stage, o, True).wait_recv()
            total = total + recv[stage][partner(stage, o)[1]]
        if out is None:
            buf[at, :] = total
        else:
            out(total)
        for o in range(1, radices[stage]):
            reduce_copy(buf, recv, ss, rs, unit, stage, o, False).wait_send()

    def gather_copy(buf, ss, rs, unit, stage, o, incoming):
        dev, d = partner(stage, o)
        w = width(unit, stage)
        digit = d if incoming else digits[stage]
        at = pl.multiple_of(base_of(unit, stage) + digit * w, 8)
        return pltpu.make_async_remote_copy(
            src_ref=buf.at[pl.ds(at, w)], dst_ref=buf.at[pl.ds(at, w)],
            send_sem=ss.at[stage, o], recv_sem=rs.at[stage, digit],
            device_id=dev, device_id_type=pl.DeviceIdType.MESH)

    for i in range(parts):
        load(0, i).wait()
        hi, lo = split(s_buf[i * step : (i + 1) * step, :])
        both = over_rows(hi, jnp.concatenate([hi, lo], axis=1))
        if i == 0:
            gacc[...] = both
        else:
            gacc[...] += both
    inv = 1.0 / (rows * count)
    for n, (p, q) in enumerate(pairs(k)):
        rp, rq = slice(p * BLK, (p + 1) * BLK), slice(q * BLK, (q + 1) * BLK)
        mid = gacc[rp, k + q * BLK : k + (q + 1) * BLK]
        mir = gacc[rq, k + p * BLK : k + (p + 1) * BLK]
        g[n * BLK : (n + 1) * BLK, :] = (gacc[rp, rq] + (mid + mir.T)) * inv
    ug = g.shape[0] // count
    gr = (g, (g1, g2, g3), send_g, recv_g, ug)
    pl.semaphore_wait(barrier, ra + rb + rc - 3)
    reduce_start(*gr, 0)

    fr = p_buf.shape[1] // count
    for i in range(parts):
        load(1, i).wait()

    def product(f0):
        acc = None
        for i in range(parts):
            at = slice(i * step, (i + 1) * step)
            hi, lo = split(s_buf[at, :])
            ph, plo = split(p_buf[at, f0 : f0 + BLK])
            both = over_rows(ph, jnp.concatenate([hi, lo], axis=1))
            t = both[:, :k] + (both[:, k:] + over_rows(plo, hi))
            acc = t if acc is None else acc + t
        for m in range(BLK // fr):
            d = f0 // fr + m
            pos = (d % ra) * (rb * rc) + ((d // ra) % rb) * rc + d // (ra * rb)
            r[pos * fr : (pos + 1) * fr, :] = acc[m * fr : (m + 1) * fr, :]

    todo = list(range(0, p_buf.shape[1], BLK))
    product(todo[0])
    reduce_end(*gr, 0)
    reduce_start(*gr, 1)
    for f0 in todo[1:]:
        product(f0)
    reduce_end(*gr, 1)
    reduce_start(*gr, 2)
    rr = (r, (r1, r2, r3), send_r, recv_r, fr)

    def put(total):
        full[pl.ds(pl.multiple_of(base_of(ug, 3), 8), ug), :] = total

    reduce_end(*gr, 2, put)

    def gather(stage, now):
        for o in range(1, radices[stage]):
            cp = gather_copy(full, send_a, recv_a, ug, stage, o, not now)
            if now:
                cp.start()
            else:
                cp.wait_recv()

    for stage in (2, 1, 0):
        gather(stage, True)
        gather(stage, False)

    reduce_start(*rr, 0)
    work[...] = jnp.zeros((k, k), jnp.float32)
    for i, (p, q) in enumerate(pairs(k)):
        work[p * BLK : (p + 1) * BLK, q * BLK : (q + 1) * BLK] = full[i * BLK : (i + 1) * BLK, :]

    def put_share(total):
        share[...] = total

    def between(p):
        @pl.when(p == 0)
        def _():
            reduce_end(*rr, 0)
            reduce_start(*rr, 1)

        @pl.when(p == 1)
        def _():
            reduce_end(*rr, 1)
            reduce_start(*rr, 2)

    inverse_factor(work, diag, dinv, between)
    reduce_end(*rr, 2, put_share)
    keep = lax.broadcasted_iota(jnp.int32, (k, k), 1) <= lax.broadcasted_iota(jnp.int32, (k, k), 0)
    inverse[...] = jnp.where(keep, work[...], 0.0)
    for stage in range(3):
        for o in range(1, radices[stage]):
            gather_copy(full, send_a, recv_a, ug, stage, o, False).wait_send()


def sums(sketch, panel, radices):
    rows, k = sketch.shape
    frames = panel.shape[1]
    ra, rb, rc = radices
    count = ra * rb * rc
    packed = len(pairs(k)) * BLK
    ug, ur = packed // count, frames // count
    parts = 4
    f32 = jnp.float32

    def slots(unit, width):
        return [
            pltpu.VMEM((ra, unit * rb * rc, width), f32),
            pltpu.VMEM((rb, unit * rc, width), f32),
            pltpu.VMEM((rc, unit, width), f32),
        ]

    most = max(radices)
    dma = pltpu.SemaphoreType.DMA
    return pl.pallas_call(
        functools.partial(sums_kernel, radices),
        out_shape=(jax.ShapeDtypeStruct((k, k), f32), jax.ShapeDtypeStruct((ur, k), f32)),
        in_specs=[pl.BlockSpec(memory_space=pl.ANY)] * 2,
        out_specs=(pl.BlockSpec(memory_space=pltpu.VMEM),) * 2,
        scratch_shapes=[
            pltpu.VMEM((k, k), f32), pltpu.VMEM((BLK, BLK), f32), pltpu.VMEM((BLK, BLK), f32),
            pltpu.VMEM((packed, BLK), f32),
            pltpu.VMEM((rows, k), f32), pltpu.VMEM((rows, frames), f32), pltpu.VMEM((k, 2 * k), f32),
            pltpu.VMEM((packed, BLK), f32), *slots(ug, BLK),
            pltpu.VMEM((frames, k), f32), *slots(ur, k),
            dma((2, parts)),
            dma((3, most)), dma((3, most)), dma((3, most)), dma((3, most)), dma((3, most)), dma((3, most)),
        ],
        compiler_params=pltpu.CompilerParams(
            collective_id=0, has_side_effects=True, vmem_limit_bytes=60 * 1024 * 1024),
    )(sketch, panel)


def factor_kernel(g_ref, inverse, work, diag, dinv):
    k = work.shape[0]
    work[...] = jnp.zeros((k, k), jnp.float32)
    for i, (p, q) in enumerate(pairs(k)):
        work[p * BLK : (p + 1) * BLK, q * BLK : (q + 1) * BLK] = g_ref[i * BLK : (i + 1) * BLK, :]
    inverse_factor(work, diag, dinv)
    keep = lax.broadcasted_iota(jnp.int32, (k, k), 1) <= lax.broadcasted_iota(jnp.int32, (k, k), 0)
    inverse[...] = jnp.where(keep, work[...], 0.0)


def factor(g, k):
    f32 = jnp.float32
    return pl.pallas_call(
        factor_kernel,
        out_shape=jax.ShapeDtypeStruct((k, k), f32),
        scratch_shapes=[pltpu.VMEM((k, k), f32), pltpu.VMEM((BLK, BLK), f32), pltpu.VMEM((BLK, BLK), f32)],
        compiler_params=pltpu.CompilerParams(vmem_limit_bytes=32 * 1024 * 1024),
    )(g)


def basis_kernel(scale, w_ref, share_ref, s_ref, basis_ref, proj_ref, wh, wl):
    n = w_ref.shape[0]

    @pl.when(pl.program_id(0) == 0)
    def _():
        w = w_ref[...]
        hi, lo = split(w)
        wh[...] = hi
        wl[...] = lo
        proj_ref[...] = scale * lax.dot_general(
            share_ref[...], w, (((1,), (1,)), ((), ())), precision=HI, preferred_element_type=jnp.float32)

    def times(x, lo, hi, depth):
        nt = (((1,), (1,)), ((), ()))
        return lax.dot_general(x[:, :depth], lo[hi, :depth], nt, preferred_element_type=jnp.float32)

    sh, sl = split(s_ref[...])
    half = n // 2
    for at, depth in ((slice(0, half), half), (slice(half, n), n)):
        small = times(sh, wl, at, depth) + times(sl, wh, at, depth)
        basis_ref[:, at] = times(sh, wh, at, depth) + small


def finish(w, share, sketch, count):
    rows, k = sketch.shape
    tile = 256
    scale = 1.0 / (rows * count) ** 0.5
    f32 = jnp.float32
    return pl.pallas_call(
        functools.partial(basis_kernel, scale),
        grid=(rows // tile,),
        out_shape=(jax.ShapeDtypeStruct((rows, k), f32), jax.ShapeDtypeStruct(share.shape, f32)),
        in_specs=[
            pl.BlockSpec(w.shape, lambda i: (0, 0)),
            pl.BlockSpec(share.shape, lambda i: (0, 0)),
            pl.BlockSpec((tile, k), lambda i: (i, 0)),
        ],
        out_specs=(pl.BlockSpec((tile, k), lambda i: (i, 0)), pl.BlockSpec(share.shape, lambda i: (0, 0))),
        scratch_shapes=[
            pltpu.VMEM((k, k), jnp.bfloat16), pltpu.VMEM((k, k), jnp.bfloat16),
        ],
        compiler_params=pltpu.CompilerParams(vmem_limit_bytes=60 * 1024 * 1024),
    )(w, share, sketch)


def plain_sums(sketch, panel):
    k = sketch.shape[1]
    total = sketch.shape[0] * lax.axis_size("rows")
    high = dict(precision=HI, preferred_element_type=jnp.float32)
    over = (((0,), (0,)), ((), ()))
    gram = lax.psum(lax.dot_general(sketch, sketch, over, **high) / total, "rows")
    share = lax.psum_scatter(lax.dot_general(panel, sketch, over, **high), "rows", scatter_dimension=0, tiled=True)
    blocks = [gram[p * BLK : (p + 1) * BLK, q * BLK : (q + 1) * BLK] for p, q in pairs(k)]
    return jnp.concatenate(blocks, axis=0), share


def on_device(sketch, panel):
    count = lax.axis_size("rows")
    k, frames = sketch.shape[1], panel.shape[1]
    packed = len(pairs(k)) * BLK
    if count % 16 == 0 and packed % (8 * count) == 0 and frames % (8 * count) == 0:
        w, share = sums(sketch, panel, (2, 8, count // 16))
    else:
        g, share = plain_sums(sketch, panel)
        w = factor(g, k)
    return finish(w, share, sketch, count)


def solution(mesh):
    return jax.shard_map(
        on_device,
        mesh=mesh,
        in_specs=(P("rows", None), P("rows", None)),
        out_specs=(P("rows", None), P("rows", None)),
        check_vma=False,
    )
```
